32 devices in a mesh: vrow: 8 (over z, x), aux: 2 (over y), grp: 2 (over core).
Axes of the slice: x: 2, y: 2, z: 4, core: 2. Of those that a mesh axis runs over, the one named last changes fastest.
Arguments:
- trials: bfloat16 [192, 3840], P(None, 'vrow'), may hold values from -6 to 6
- vv_factors: bfloat16 [16, 3840, 3840], P(('aux', 'grp'), 'vrow'), may hold values from -0.09375 to 0.09375
- screened: bfloat16 [16, 96, 96], P(('aux', 'grp')), may hold values from -0.15625 to 0.15625
- ov_factors: bfloat16 [16, 3840, 96], P(('aux', 'grp'), 'vrow'), may hold values from -0.078125 to 0.078125
- occ_energy: float32 [96], replicated, may hold values from -1.5 to -0.3
- virt_energy: float32 [3840], replicated, may hold values from 0.2 to 2.5
- occ_order: int32 [96], replicated, may hold values from 0 to 95, each once
- virt_order: int32 [3840], P('vrow'), may hold values from 0 to 3839, each once
Outputs:
- sigma: float32 [192, 3840], P(('aux', 'grp'), 'vrow')
The draws below stay inside these ranges and needn't reach their ends.
Inputs may be any that keep to these rules, and one draw needn't show every extreme that they name: `occ_order`: each active occupied orbital names a different entry. `virt_order`: each virtual orbital names a different entry.
All inputs are finite; a program needn't handle non-finite values.
Results may differ from the reference program's by a relative error of at most 0.0022.
Values may be sent and summed in bfloat16 or wider, within the bound.
A program may use at most 64 MiB of HBM per device.

```python
import jax
import jax.numpy as jnp
from jax import lax

NO = 96
NV = 3840
NTR = 2
WIN = 16


def shard_levels(key, extent, shards, low, largest):
    factor_of = 1.0
    for dim, parts in shards:
        heights = jax.random.uniform(jax.random.fold_in(jax.random.fold_in(key, 6), dim), (parts,), jnp.float32, low / len(shards), largest / len(shards))
        factor_of = factor_of * jnp.repeat(jnp.exp(heights), extent[dim] // parts).reshape((-1,) + (1,) * (len(extent) - 1 - dim))
    return factor_of


def gaussian(rng, dims, scale, limit, split=(), held_as=jnp.bfloat16):
    level = shard_levels(rng, dims, split, -0.22, 0.18) if split else 1.0
    drawn = jax.random.normal(rng, dims, jnp.float32) * scale * level
    return jnp.minimum(jnp.maximum(drawn, -limit), limit).astype(held_as)


def setup_inputs(seed: int = 0) -> dict:
    key_of = jax.random.split(jax.random.key(seed), 9)
    trials = gaussian(key_of[0], (NTR * NO, NV), 1.0, 6.0, ((1, 8),))
    vv_factors = gaussian(key_of[1], (WIN, NV, NV), NV ** -0.5, 0.09375, ((0, 4), (1, 8)))
    screened = gaussian(key_of[2], (WIN, NO, NO), (NO * WIN) ** -0.5, 0.15625, ((0, 4),))
    ov_factors = gaussian(key_of[3], (WIN, NV, NO), (2 * (WIN * NO * NV) ** 0.5) ** -0.5, 0.078125, ((0, 4), (1, 8)))
    occ_energy = jnp.clip(jax.random.uniform(key_of[4], (NO,), jnp.float32, -1.5, -0.3), -1.5, -0.3)
    virt_energy = jnp.clip(jax.random.uniform(key_of[5], (NV,), jnp.float32, 0.2, 2.5), 0.2, 2.5)
    occ_order = jax.random.permutation(key_of[6], NO).astype(jnp.int32)
    virt_order = jax.random.permutation(key_of[7], NV).astype(jnp.int32)
    return {"trials": trials, "vv_factors": vv_factors, "screened": screened, "ov_factors": ov_factors, "occ_energy": occ_energy, "virt_energy": virt_energy, "occ_order": occ_order, "virt_order": virt_order}


def reference(trials, vv_factors, screened, ov_factors, occ_energy, virt_energy, occ_order, virt_order):
    occupied = occ_energy.shape[0]
    count_trials = trials.shape[0] // occupied
    trials_wide = trials.astype(jnp.float32)
    split_trials = trials_wide.reshape(count_trials, occupied, NV)
    factors_wide = ov_factors.astype(jnp.float32)
    pair_sums = jnp.einsum("qai,tia->qt", factors_wide, split_trials)
    exchange_term = 2.0 * jnp.einsum("qai,qt->tia", factors_wide, pair_sums)

    def add_function(running, inputs):
        factor_slab, screen = inputs
        product = jnp.dot(trials, factor_slab.T, preferred_element_type=jnp.float32).astype(jnp.bfloat16)
        shaped = product.astype(jnp.float32).reshape(count_trials, occupied, NV)
        return running + jnp.einsum("ji,tja->tia", screen.astype(jnp.float32), shaped), None

    direct_term, unused = lax.scan(add_function, jnp.zeros((count_trials, occupied, NV), jnp.float32), (vv_factors, screened))
    virt_levels = virt_energy[virt_order.astype(jnp.int32)]
    occ_levels = occ_energy[occ_order.astype(jnp.int32)]
    differences = virt_levels[None, :] - jnp.tile(occ_levels, count_trials)[:, None]
    combined = (exchange_term - direct_term).reshape(count_trials * occupied, NV)
    return differences * trials_wide + combined
```

```python
import functools

import jax
import jax.numpy as jnp
from jax import lax
from jax.experimental import pallas as pl
from jax.experimental.pallas import tpu as pltpu
from jax.sharding import PartitionSpec as P

MESH = pl.DeviceIdType.MESH
F32 = jnp.float32
BF16 = jnp.bfloat16
LANES = 128
PACK = 16


def table_lookup(order, table):
    columns = lax.broadcasted_iota(jnp.int32, (order.shape[0], table.shape[0]), 1)
    picker = (order[:, None] == columns).astype(jnp.float32)
    return jnp.dot(picker, table, precision=lax.Precision.HIGHEST)


def plain_on_device(
    trials, vv_factors, screened, ov_factors, occ_energy, virt_energy, occ_order, virt_order
):
    groups = lax.axis_size(("aux", "grp"))
    rows_all = trials.shape[0]
    occupied = occ_energy.shape[0]
    count_trials = rows_all // occupied
    local_virt = trials.shape[1]
    slab_count = vv_factors.shape[0]
    row_share = rows_all // groups
    row_offset = lax.axis_index(("aux", "grp")) * row_share
    split_trials = trials.reshape(count_trials, occupied, local_virt)
    partial_pairs = jnp.einsum(
        "qai,tia->qt", ov_factors, split_trials, preferred_element_type=jnp.float32
    )
    pair_sums = lax.psum(partial_pairs, "vrow")
    exchange_term = 2.0 * jnp.einsum("qai,qt->tia", ov_factors.astype(jnp.float32), pair_sums)
    products = jnp.einsum(
        "rb,qab->qra",
        lax.all_gather(trials, "vrow", axis=1, tiled=True),
        vv_factors,
        preferred_element_type=jnp.float32,
    )
    rounded = products.astype(jnp.bfloat16).reshape(slab_count, count_trials, occupied, local_virt)
    direct_term = jnp.einsum("qji,qtja->tia", screened, rounded, preferred_element_type=jnp.float32)
    combined = (exchange_term - direct_term).reshape(rows_all, local_virt)
    summed = lax.psum_scatter(combined, ("aux", "grp"), scatter_dimension=0, tiled=True)
    virt_levels = table_lookup(virt_order, virt_energy)
    occ_levels = table_lookup(occ_order, occ_energy)
    row_ids = row_offset + lax.broadcasted_iota(jnp.int32, (row_share,), 0)
    row_levels = table_lookup(row_ids % occupied, occ_levels)
    own_trials = lax.dynamic_slice_in_dim(trials, row_offset, row_share, 0).astype(jnp.float32)
    return summed + (virt_levels[None, :] - row_levels[:, None]) * own_trials


def fused_kernel(
    trials, vv_hbm, screened, ov_hbm, occ_energy, virt_energy, occ_order, virt_order,
    out,
    gathered, packed, vbuf, ovbuf, acc, screen_bd, combined, pair_buf, send_buf, recv_buf,
    vv_sem, ov_sem, z_send, z_recv, x_send, x_recv, y_send, y_recv, c_send, c_recv,
    p_send, p_recv, r_send, r_recv,
):
    rows, local = trials.shape
    slabs = vv_hbm.shape[0]
    occupied = occ_energy.shape[1]
    count_trials = rows // occupied
    half_cols = packed.shape[2]
    quarter = rows // 4
    half_rows = rows // 2
    levels = gathered.shape[0] // 2

    v = lax.axis_index("vrow")
    y = lax.axis_index("aux")
    c = lax.axis_index("grp")
    z = v // 2
    x = v % 2
    half = z // 2
    partner_z = {0: z, 1: z + 1 - 2 * (z % 2), 2: (z + 2) % 4, 3: 3 - z}

    def row_id(zz, xx):
        return zz * 2 + xx

    mine = pl.ds(pl.multiple_of((2 * c + y) * quarter, PACK), quarter)
    my_half = pl.ds(pl.multiple_of(c * half_rows, PACK), half_rows)

    vv_copies = {}
    for slot in range(2):
        side = half if slot == 0 else 1 - half
        cols = pl.ds(pl.multiple_of(side * half_cols, LANES), half_cols)
        for q in range(slabs):
            vv_copies[slot, q] = pltpu.make_async_copy(
                vv_hbm.at[q, :, cols], vbuf.at[slot, q], vv_sem.at[slot, q]
            )
    ov_copy = pltpu.make_async_copy(ov_hbm, ovbuf, ov_sem)
    ov_copy.start()
    for q in range(slabs):
        vv_copies[0, q].start()
    for q in range(slabs):
        vv_copies[1, q].start()

    barrier = pltpu.get_barrier_semaphore()
    peers = [(row_id(partner_z[d], xx), y, c) for d in range(4) for xx in (x, 1 - x)][1:]
    group = [(v, 1 - y, c), (v, y, 1 - c), (v, 1 - y, 1 - c)]
    for peer in peers + group:
        pl.semaphore_signal(barrier, inc=1, device_id=peer, device_id_type=MESH)
    pl.semaphore_wait(barrier, len(peers) + len(group))

    def remote(src, dst, send, recv, peer):
        return pltpu.make_async_remote_copy(
            src_ref=src, dst_ref=dst, send_sem=send, recv_sem=recv,
            device_id=peer, device_id_type=MESH,
        )

    z_copies, x_copies, y_copies, c_copies = {}, {}, {}, {}
    to_x = (row_id(z, 1 - x), y, c)
    to_y = (v, 1 - y, c)
    to_c = (v, y, 1 - c)
    for d in (1, 2, 3):
        z_copies[d] = remote(
            trials.at[mine], gathered.at[v, mine], z_send.at[d], z_recv.at[d],
            (row_id(partner_z[d], x), y, c),
        )
    x_copies[0] = remote(
        trials.at[my_half], gathered.at[v, my_half], x_send.at[0], x_recv.at[0], to_x
    )
    for d in (1, 2, 3):
        same = gathered.at[row_id(partner_z[d], x)]
        cross = gathered.at[row_id(partner_z[d], 1 - x)]
        x_copies[d] = remote(same.at[mine], same.at[mine], x_send.at[d], x_recv.at[d], to_x)
        for k, block in ((0, same), (1, cross)):
            y_copies[d, k] = remote(
                block.at[mine], block.at[mine], y_send.at[d, k], y_recv.at[d, k], to_y
            )
            c_copies[d, k] = remote(
                block.at[my_half], block.at[my_half], c_send.at[d, k], c_recv.at[d, k], to_c
            )
    cross = gathered.at[row_id(z, 1 - x)]
    c_copies[0, 1] = remote(
        cross.at[my_half], cross.at[my_half], c_send.at[0, 1], c_recv.at[0, 1], to_c
    )

    for d in (3, 2, 1):
        z_copies[d].start()
    x_copies[0].start()

    gathered[v] = trials[...]
    ov_copy.wait()
    split = [trials[t * occupied:(t + 1) * occupied, :].astype(F32) for t in range(count_trials)]
    whole = (local // LANES) * LANES
    pair_rows = []
    for q in range(slabs):
        factor = ovbuf[q].astype(F32)
        for t in range(count_trials):
            pair_rows.append(jnp.sum(factor * split[t], axis=0, keepdims=True))
    pair_buf[0] = jnp.concatenate(pair_rows, axis=0)
    p_copies = []
    for k, peer in enumerate(peers):
        p_copies.append(
            remote(pair_buf.at[0], pair_buf.at[k + 1], p_send.at[k], p_recv.at[k], peer)
        )
        p_copies[-1].start()

    for d in (1, 2, 3):
        z_copies[d].wait_recv()
        x_copies[d].start()
        y_copies[d, 0].start()

    screen_bd[...] = jnp.zeros(screen_bd.shape, screen_bd.dtype)
    for q in range(slabs):
        turned = screened[q].astype(F32).T.astype(BF16)
        for t in range(count_trials):
            span = slice(t * occupied, (t + 1) * occupied)
            screen_bd[q, span, span] = turned

    x_copies[0].wait_recv()
    c_copies[0, 1].start()
    for d in (1, 2, 3):
        x_copies[d].wait_recv()
        y_copies[d, 1].start()

    blocks = virt_energy.shape[0]
    order = virt_order[...]
    picker = (order // LANES == lax.broadcasted_iota(jnp.int32, (blocks, local), 0)).astype(F32)
    rows_of = lax.dot_general(
        virt_energy[...].T, picker, (((1,), (0,)), ((), ())),
        precision=lax.Precision.HIGHEST, preferred_element_type=F32,
    )
    lane_ids = lax.broadcasted_iota(jnp.int32, (LANES, local), 0)
    virt_levels = jnp.sum(
        jnp.where(order % LANES == lane_ids, rows_of, 0.0), axis=0, keepdims=True
    )
    share = out.shape[0]
    owner = 2 * y + c
    row_ids = owner * share + lax.broadcasted_iota(jnp.int32, (share, occupied), 0)
    row_ids = row_ids % occupied
    occ_ids = lax.broadcasted_iota(jnp.int32, (share, occupied), 1)
    order_of = jnp.sum(
        jnp.where(row_ids == occ_ids, occ_order[...].astype(F32), 0.0), axis=1, keepdims=True
    ).astype(jnp.int32)
    row_levels = jnp.sum(
        jnp.where(order_of == occ_ids, occ_energy[...], 0.0), axis=1, keepdims=True
    )
    own_rows = pl.ds(pl.multiple_of(owner * share, PACK), share)
    out[...] = (virt_levels - row_levels) * trials[own_rows, :].astype(F32)

    y_copies[1, 0].wait_recv()
    c_copies[1, 0].start()
    y_copies[1, 1].wait_recv()
    c_copies[1, 1].start()

    for copy in p_copies:
        copy.wait_recv()
    pair_sums = 2.0 * jnp.sum(jnp.sum(pair_buf[...], axis=0), axis=1, keepdims=True)
    for t in range(count_trials):
        term = jnp.zeros((occupied, local), F32)
        for q in range(slabs):
            k = q * count_trials + t
            term = term + ovbuf[q].astype(F32) * pair_sums[k:k + 1, :]
        combined[t * occupied:(t + 1) * occupied, :] = term

    def pack(slot):
        side = half if slot == 0 else 1 - half
        for s in range(half_cols // local):
            packed[slot, :, s * local:(s + 1) * local] = gathered[side * (levels) + s]

    def product(slot, q):
        return lax.dot_general(
            vbuf[slot, q], packed[slot], (((1,), (1,)), ((), ())), preferred_element_type=F32
        )

    for d in (2, 3):
        for k in (0, 1):
            y_copies[d, k].wait_recv()
            c_copies[d, k].start()
    c_copies[0, 1].wait_recv()
    c_copies[1, 0].wait_recv()
    c_copies[1, 1].wait_recv()
    pack(0)
    for q in range(slabs):
        vv_copies[0, q].wait()
        acc[q] = product(0, q)

    for d in (2, 3):
        for k in (0, 1):
            c_copies[d, k].wait_recv()
    pack(1)
    total = combined[...]
    for q in range(slabs):
        vv_copies[1, q].wait()
        image = (acc[q] + product(1, q)).astype(BF16)
        total = total - lax.dot_general(
            screen_bd[q], image, (((1,), (1,)), ((), ())), preferred_element_type=F32
        )
    combined[...] = total

    r_copies = []
    for k, (yy, cc) in enumerate(((1 - y, 1 - c), (1 - y, c), (y, 1 - c))):
        theirs = pl.ds(pl.multiple_of((2 * yy + cc) * share, PACK), share)
        send_buf[k] = combined[theirs, :].astype(BF16)
        r_copies.append(
            remote(send_buf.at[k], recv_buf.at[k], r_send.at[k], r_recv.at[k], (v, yy, cc))
        )
        r_copies[-1].start()
    summed = out[...] + combined[own_rows, :]
    for k in (2, 1, 0):
        r_copies[k].wait_recv()
        summed = summed + recv_buf[k].astype(F32)
    out[...] = summed

    everything = [*z_copies.values(), *x_copies.values(), *y_copies.values(), *c_copies.values()]
    for copy in everything + p_copies + r_copies:
        copy.wait_send()


def fused_on_device(
    trials, vv_factors, screened, ov_factors, occ_energy, virt_energy, occ_order, virt_order
):
    rows, local = trials.shape
    slabs, _, virt = vv_factors.shape
    occupied = occ_energy.shape[0]
    count_trials = rows // occupied
    parts = virt // local
    share = rows // 4
    vmem = pl.BlockSpec(memory_space=pltpu.VMEM)
    anywhere = pl.BlockSpec(memory_space=pl.ANY)
    dma = pltpu.SemaphoreType.DMA
    return pl.pallas_call(
        fused_kernel,
        out_shape=jax.ShapeDtypeStruct((share, local), F32),
        in_specs=[vmem, anywhere, vmem, anywhere, vmem, vmem, vmem, vmem],
        out_specs=vmem,
        scratch_shapes=[
            pltpu.VMEM((parts, rows, local), BF16),
            pltpu.VMEM((2, rows, virt // 2), BF16),
            pltpu.VMEM((2, slabs, local, virt // 2), BF16),
            pltpu.VMEM((slabs, occupied, local), BF16),
            pltpu.VMEM((slabs, local, rows), F32),
            pltpu.VMEM((slabs, rows, rows), BF16),
            pltpu.VMEM((rows, local), F32),
            pltpu.VMEM((parts, slabs * count_trials, local), F32),
            pltpu.VMEM((3, share, local), BF16),
            pltpu.VMEM((3, share, local), BF16),
            dma((2, slabs)), dma,
            dma((4,)), dma((4,)), dma((4,)), dma((4,)),
            dma((4, 2)), dma((4, 2)), dma((4, 2)), dma((4, 2)),
            dma((parts - 1,)), dma((parts - 1,)), dma((3,)), dma((3,)),
        ],
        compiler_params=pltpu.CompilerParams(
            collective_id=0, has_side_effects=True, vmem_limit_bytes=56 * 1024 * 1024
        ),
    )(
        trials,
        vv_factors,
        screened,
        jnp.swapaxes(ov_factors, 1, 2),
        occ_energy.reshape(1, occupied),
        virt_energy.reshape(virt // LANES, LANES),
        occ_order.reshape(1, occupied),
        virt_order.reshape(1, local),
    )


def on_device(trials, vv_factors, *rest):
    rows, local = trials.shape
    virt = vv_factors.shape[2]
    sizes = [lax.axis_size(name) for name in ("vrow", "aux", "grp")]
    fits = (
        sizes == [8, 2, 2]
        and rows % (4 * PACK) == 0
        and (virt // 2) % LANES == 0
        and virt == sizes[0] * local
    )
    body = fused_on_device if fits else plain_on_device
    return body(trials, vv_factors, *rest)


def solution(mesh):
    placed = (
        P(None, "vrow"),
        P(("aux", "grp"), "vrow", None),
        P(("aux", "grp"), None, None),
        P(("aux", "grp"), "vrow", None),
        P(),
        P(),
        P(),
        P("vrow"),
    )
    return jax.shard_map(
        on_device, mesh=mesh, in_specs=placed, out_specs=P(("aux", "grp"), "vrow"), check_vma=False
    )
```

```python
import functools

import jax
import jax.numpy as jnp
from jax import lax
from jax.experimental import pallas as pl
from jax.experimental.pallas import tpu as pltpu
from jax.sharding import PartitionSpec as P

MESH = pl.DeviceIdType.MESH
F32 = jnp.float32
BF16 = jnp.bfloat16
LANES = 128
PACK = 16


def table_lookup(order, table):
    columns = lax.broadcasted_iota(jnp.int32, (order.shape[0], table.shape[0]), 1)
    picker = (order[:, None] == columns).astype(jnp.float32)
    return jnp.dot(picker, table, precision=lax.Precision.HIGHEST)


def plain_on_device(
    trials, vv_factors, screened, ov_factors, occ_energy, virt_energy, occ_order, virt_order
):
    groups = lax.axis_size(("aux", "grp"))
    rows_all = trials.shape[0]
    occupied = occ_energy.shape[0]
    count_trials = rows_all // occupied
    local_virt = trials.shape[1]
    slab_count = vv_factors.shape[0]
    row_share = rows_all // groups
    row_offset = lax.axis_index(("aux", "grp")) * row_share
    split_trials = trials.reshape(count_trials, occupied, local_virt)
    partial_pairs = jnp.einsum(
        "qai,tia->qt", ov_factors, split_trials, preferred_element_type=jnp.float32
    )
    pair_sums = lax.psum(partial_pairs, "vrow")
    exchange_term = 2.0 * jnp.einsum("qai,qt->tia", ov_factors.astype(jnp.float32), pair_sums)
    products = jnp.einsum(
        "rb,qab->qra",
        lax.all_gather(trials, "vrow", axis=1, tiled=True),
        vv_factors,
        preferred_element_type=jnp.float32,
    )
    rounded = products.astype(jnp.bfloat16).reshape(slab_count, count_trials, occupied, local_virt)
    direct_term = jnp.einsum("qji,qtja->tia", screened, rounded, preferred_element_type=jnp.float32)
    combined = (exchange_term - direct_term).reshape(rows_all, local_virt)
    summed = lax.psum_scatter(combined, ("aux", "grp"), scatter_dimension=0, tiled=True)
    virt_levels = table_lookup(virt_order, virt_energy)
    occ_levels = table_lookup(occ_order, occ_energy)
    row_ids = row_offset + lax.broadcasted_iota(jnp.int32, (row_share,), 0)
    row_levels = table_lookup(row_ids % occupied, occ_levels)
    own_trials = lax.dynamic_slice_in_dim(trials, row_offset, row_share, 0).astype(jnp.float32)
    return summed + (virt_levels[None, :] - row_levels[:, None]) * own_trials


def fused_kernel(
    trials_hbm, vv_hbm, screened_hbm, ov_hbm, occ_e_hbm, virt_e_hbm, occ_o_hbm, virt_o_hbm,
    out,
    screened, occ_energy, virt_energy, occ_order, virt_order,
    gathered, packed, vbuf, ovbuf, acc, screen_bd, combined, pair_buf, send_buf, recv_buf,
    vv_sem, in_sem, z_send, z_recv, x_send, x_recv, y_send, y_recv, c_send, c_recv,
    p_send, p_recv, r_send, r_recv,
):
    rows, local = trials_hbm.shape
    slabs = vv_hbm.shape[0]
    occupied = occ_energy.shape[1]
    count_trials = rows // occupied
    half_cols = packed.shape[2]
    quarter = rows // 4
    half_rows = rows // 2
    levels = gathered.shape[0] // 2

    v = lax.axis_index("vrow")
    y = lax.axis_index("aux")
    c = lax.axis_index("grp")
    z = v // 2
    x = v % 2
    half = z // 2
    partner_z = {0: z, 1: z + 1 - 2 * (z % 2), 2: (z + 2) % 4, 3: 3 - z}

    def row_id(zz, xx):
        return zz * 2 + xx

    mine = pl.ds(pl.multiple_of((2 * c + y) * quarter, PACK), quarter)
    my_half = pl.ds(pl.multiple_of(c * half_rows, PACK), half_rows)

    barrier = pltpu.get_barrier_semaphore()
    peers = [(row_id(partner_z[d], xx), y, c) for d in range(4) for xx in (x, 1 - x)][1:]
    group = [(v, 1 - y, c), (v, y, 1 - c), (v, 1 - y, 1 - c)]
    for peer in peers + group:
        pl.semaphore_signal(barrier, inc=1, device_id=peer, device_id_type=MESH)

    vv_copies = {}
    for slot in range(2):
        side = half if slot == 0 else 1 - half
        cols = pl.ds(pl.multiple_of(side * half_cols, LANES), half_cols)
        for q in range(slabs):
            vv_copies[slot, q] = pltpu.make_async_copy(
                vv_hbm.at[q, :, cols], vbuf.at[slot, q], vv_sem.at[slot, q]
            )
    trials = gathered.at[v]
    in_copies = [
        pltpu.make_async_copy(src, dst, in_sem.at[k])
        for k, (src, dst) in enumerate((
            (trials_hbm, trials), (ov_hbm, ovbuf), (screened_hbm, screened),
            (occ_e_hbm, occ_energy), (virt_e_hbm, virt_energy),
            (occ_o_hbm, occ_order), (virt_o_hbm, virt_order),
        ))
    ]
    for copy in in_copies:
        copy.start()
    for q in range(slabs):
        vv_copies[0, q].start()
    for q in range(slabs):
        vv_copies[1, q].start()

    pl.semaphore_wait(barrier, len(peers) + len(group))

    def remote(src, dst, send, recv, peer):
        return pltpu.make_async_remote_copy(
            src_ref=src, dst_ref=dst, send_sem=send, recv_sem=recv,
            device_id=peer, device_id_type=MESH,
        )

    z_copies, x_copies, y_copies, c_copies = {}, {}, {}, {}
    to_x = (row_id(z, 1 - x), y, c)
    to_y = (v, 1 - y, c)
    to_c = (v, y, 1 - c)
    for d in (1, 2, 3):
        z_copies[d] = remote(
            trials_hbm.at[mine], gathered.at[v, mine], z_send.at[d], z_recv.at[d],
            (row_id(partner_z[d], x), y, c),
        )
    x_copies[0] = remote(
        trials_hbm.at[my_half], gathered.at[v, my_half], x_send.at[0], x_recv.at[0], to_x
    )
    for d in (1, 2, 3):
        same = gathered.at[row_id(partner_z[d], x)]
        cross = gathered.at[row_id(partner_z[d], 1 - x)]
        x_copies[d] = remote(same.at[mine], same.at[mine], x_send.at[d], x_recv.at[d], to_x)
        for k, block in ((0, same), (1, cross)):
            y_copies[d, k] = remote(
                block.at[mine], block.at[mine], y_send.at[d, k], y_recv.at[d, k], to_y
            )
            c_copies[d, k] = remote(
                block.at[my_half], block.at[my_half], c_send.at[d, k], c_recv.at[d, k], to_c
            )
    cross = gathered.at[row_id(z, 1 - x)]
    c_copies[0, 1] = remote(
        cross.at[my_half], cross.at[my_half], c_send.at[0, 1], c_recv.at[0, 1], to_c
    )

    for d in (3, 2, 1):
        z_copies[d].start()
    x_copies[0].start()

    for copy in in_copies:
        copy.wait()
    split = [trials[t * occupied:(t + 1) * occupied, :].astype(F32) for t in range(count_trials)]
    pair_rows = []
    for q in range(slabs):
        factor = ovbuf[q].astype(F32)
        for t in range(count_trials):
            pair_rows.append(jnp.sum(factor * split[t], axis=0, keepdims=True))
    row_sums = jnp.sum(jnp.concatenate(pair_rows, axis=0), axis=1, keepdims=True)
    pair_buf[0] = jnp.broadcast_to(row_sums, pair_buf.shape[1:])
    p_copies = []
    for k, peer in enumerate(peers):
        p_copies.append(
            remote(pair_buf.at[0], pair_buf.at[k + 1], p_send.at[k], p_recv.at[k], peer)
        )
        p_copies[-1].start()

    z_copies[1].wait_recv()
    x_copies[1].start()
    y_copies[1, 0].start()
    x_copies[0].wait_recv()
    c_copies[0, 1].start()
    for d in (2, 3):
        z_copies[d].wait_recv()
        x_copies[d].start()
        y_copies[d, 0].start()
    for d in (1, 2, 3):
        x_copies[d].wait_recv()
        y_copies[d, 1].start()

    screen_bd[...] = jnp.zeros(screen_bd.shape, screen_bd.dtype)
    for q in range(slabs):
        turned = screened[q].astype(F32).T.astype(BF16)
        for t in range(count_trials):
            span = slice(t * occupied, (t + 1) * occupied)
            screen_bd[q, span, span] = turned

    for k in (0, 1):
        y_copies[1, k].wait_recv()
        c_copies[1, k].start()

    blocks = virt_energy.shape[0]
    order = virt_order[...]
    picker = (order // LANES == lax.broadcasted_iota(jnp.int32, (blocks, local), 0)).astype(F32)
    rows_of = lax.dot_general(
        virt_energy[...].T, picker, (((1,), (0,)), ((), ())),
        precision=lax.Precision.HIGHEST, preferred_element_type=F32,
    )
    lane_ids = lax.broadcasted_iota(jnp.int32, (LANES, local), 0)
    virt_levels = jnp.sum(
        jnp.where(order % LANES == lane_ids, rows_of, 0.0), axis=0, keepdims=True
    )
    share = out.shape[0]
    owner = 2 * y + c
    row_ids = owner * share + lax.broadcasted_iota(jnp.int32, (share, occupied), 0)
    row_ids = row_ids % occupied
    occ_ids = lax.broadcasted_iota(jnp.int32, (share, occupied), 1)
    order_of = jnp.sum(
        jnp.where(row_ids == occ_ids, occ_order[...].astype(F32), 0.0), axis=1, keepdims=True
    ).astype(jnp.int32)
    row_levels = jnp.sum(
        jnp.where(order_of == occ_ids, occ_energy[...], 0.0), axis=1, keepdims=True
    )
    own_rows = pl.ds(pl.multiple_of(owner * share, PACK), share)
    out[...] = (virt_levels - row_levels) * trials[own_rows, :].astype(F32)

    for d in (2, 3):
        y_copies[d, 0].wait_recv()
        c_copies[d, 0].start()

    for copy in p_copies:
        copy.wait_recv()
    pair_sums = 2.0 * jnp.sum(pair_buf[...], axis=0)[:, :1]
    for t in range(count_trials):
        term = jnp.zeros((occupied, local), F32)
        for q in range(slabs):
            k = q * count_trials + t
            term = term + ovbuf[q].astype(F32) * pair_sums[k:k + 1, :]
        combined[t * occupied:(t + 1) * occupied, :] = term

    def pack(slot):
        side = half if slot == 0 else 1 - half
        for s in range(half_cols // local):
            packed[slot, :, s * local:(s + 1) * local] = gathered[side * (levels) + s]

    def product(slot, q):
        return lax.dot_general(
            packed[slot], vbuf[slot, q], (((1,), (1,)), ((), ())), preferred_element_type=F32
        )

    c_copies[0, 1].wait_recv()
    c_copies[1, 0].wait_recv()
    c_copies[1, 1].wait_recv()
    pack(0)
    for q in range(slabs):
        vv_copies[0, q].wait()
        acc[q] = product(0, q)
        if q < 2:
            y_copies[q + 2, 1].wait_recv()
            c_copies[q + 2, 1].start()

    for d in (2, 3):
        for k in (0, 1):
            c_copies[d, k].wait_recv()
    pack(1)
    total = combined[...]
    for q in range(slabs):
        vv_copies[1, q].wait()
        image = (acc[q] + product(1, q)).astype(BF16)
        total = total - lax.dot_general(
            screen_bd[q], image, (((1,), (0,)), ((), ())), preferred_element_type=F32
        )
    combined[...] = total

    r_copies = []
    for k, (yy, cc) in enumerate(((1 - y, 1 - c), (1 - y, c), (y, 1 - c))):
        theirs = pl.ds(pl.multiple_of((2 * yy + cc) * share, PACK), share)
        send_buf[k] = combined[theirs, :].astype(BF16)
        r_copies.append(
            remote(send_buf.at[k], recv_buf.at[k], r_send.at[k], r_recv.at[k], (v, yy, cc))
        )
        r_copies[-1].start()
    summed = out[...] + combined[own_rows, :]
    for k in (2, 1, 0):
        r_copies[k].wait_recv()
        summed = summed + recv_buf[k].astype(F32)
    out[...] = summed

    everything = [*z_copies.values(), *x_copies.values(), *y_copies.values(), *c_copies.values()]
    for copy in everything + p_copies + r_copies:
        copy.wait_send()


def fused_on_device(
    trials, vv_factors, screened, ov_factors, occ_energy, virt_energy, occ_order, virt_order
):
    rows, local = trials.shape
    slabs, _, virt = vv_factors.shape
    occupied = occ_energy.shape[0]
    count_trials = rows // occupied
    parts = virt // local
    share = rows // 4
    vmem = pl.BlockSpec(memory_space=pltpu.VMEM)
    anywhere = pl.BlockSpec(memory_space=pl.ANY)
    dma = pltpu.SemaphoreType.DMA
    return pl.pallas_call(
        fused_kernel,
        out_shape=jax.ShapeDtypeStruct((share, local), F32),
        in_specs=[anywhere] * 8,
        out_specs=vmem,
        scratch_shapes=[
            pltpu.VMEM((slabs, occupied, occupied), BF16),
            pltpu.VMEM((1, occupied), F32),
            pltpu.VMEM((virt // LANES, LANES), F32),
            pltpu.VMEM((1, occupied), jnp.int32),
            pltpu.VMEM((1, local), jnp.int32),
            pltpu.VMEM((parts, rows, local), BF16),
            pltpu.VMEM((2, rows, virt // 2), BF16),
            pltpu.VMEM((2, slabs, local, virt // 2), BF16),
            pltpu.VMEM((slabs, occupied, local), BF16),
            pltpu.VMEM((slabs, rows, local), F32),
            pltpu.VMEM((slabs, rows, rows), BF16),
            pltpu.VMEM((rows, local), F32),
            pltpu.VMEM((parts, slabs * count_trials, LANES), F32),
            pltpu.VMEM((3, share, local), BF16),
            pltpu.VMEM((3, share, local), BF16),
            dma((2, slabs)), dma((7,)),
            dma((4,)), dma((4,)), dma((4,)), dma((4,)),
            dma((4, 2)), dma((4, 2)), dma((4, 2)), dma((4, 2)),
            dma((parts - 1,)), dma((parts - 1,)), dma((3,)), dma((3,)),
        ],
        compiler_params=pltpu.CompilerParams(
            collective_id=0, has_side_effects=True, vmem_limit_bytes=56 * 1024 * 1024
        ),
    )(
        trials,
        vv_factors,
        screened,
        jnp.swapaxes(ov_factors, 1, 2),
        occ_energy.reshape(1, occupied),
        virt_energy.reshape(virt // LANES, LANES),
        occ_order.reshape(1, occupied),
        virt_order.reshape(1, local),
    )


def on_device(trials, vv_factors, *rest):
    rows, local = trials.shape
    virt = vv_factors.shape[2]
    sizes = [lax.axis_size(name) for name in ("vrow", "aux", "grp")]
    fits = (
        sizes == [8, 2, 2]
        and vv_factors.shape[0] >= 2
        and rows % (4 * PACK) == 0
        and (virt // 2) % LANES == 0
        and virt == sizes[0] * local
    )
    body = fused_on_device if fits else plain_on_device
    return body(trials, vv_factors, *rest)


def solution(mesh):
    placed = (
        P(None, "vrow"),
        P(("aux", "grp"), "vrow", None),
        P(("aux", "grp"), None, None),
        P(("aux", "grp"), "vrow", None),
        P(),
        P(),
        P(),
        P("vrow"),
    )
    return jax.shard_map(
        on_device, mesh=mesh, in_specs=placed, out_specs=P(("aux", "grp"), "vrow"), check_vma=False
    )
```
